32 devices in a mesh: seq: 16 (over z, y, x), head: 2 (over core).
Axes of the slice: x: 2, y: 2, z: 4, core: 2. Of those that a mesh axis runs over, the one named last changes fastest.
Arguments:
- ssm_input: bfloat16 [16384, 4096], P('seq', 'head'), may hold values from -125 to 125
- gate_input: bfloat16 [16384, 4096], P('seq', 'head'), may hold values from -8 to 8
- write_proj: bfloat16 [16384, 128], P('seq'), may hold values from -0.1875 to 0.1875
- read_proj: bfloat16 [16384, 128], P('seq'), may hold values from -0.5 to 0.5
- decay_codes: int32 [32, 16384], P('head', 'seq'), may hold values from 1 to 32768
- decay_rate: float32 [32], P('head'), may hold values from 0.8 to 6000
- skip_gain: float32 [32], P('head'), may hold values from 0.5 to 1.5
- norm_gain: float32 [4096], P('head'), may hold values from 0.5 to 1.5
Outputs:
- mamba_out: bfloat16 [16384, 4096], P('seq', 'head')
The draws below stay inside these ranges and needn't reach their ends.
All inputs are finite; a program needn't handle non-finite values.
Results may differ from the reference program's by a relative error of at most 0.0054.
Values sent between devices are 32-bit elements; how exact they have to be, the bound alone decides.
A program may use at most 64 MiB of HBM per device.

```python
import jax
import jax.numpy as jnp
from jax import lax

HEADS = 32
HEAD_DIM = 128
STATE = 128
GROUP = 256
TOK_DEV = 1024
TOKENS = 16384


def draw_ssm_input(key, part):
    first = jax.random.fold_in(key, 0)
    third = jax.random.fold_in(key, 2)
    width = HEADS * HEAD_DIM
    columns = jnp.arange(width, dtype=jnp.float32) / width
    base = jnp.clip(jax.random.normal(first, (TOKENS, width), jnp.float32), -5.0, 5.0)
    row_scale = 10.0 ** jax.random.uniform(third, (TOKENS, 1), jnp.float32)
    values = base * row_scale * 10.0 ** columns[None, :] / 4.0
    return values.astype(jnp.bfloat16)


def draw_decay_rate(key, part):
    first, second, third = jax.random.split(key, 3)
    slow_rate = 0.8 * 3.0 ** jax.random.uniform(first, (HEADS,), jnp.float32)
    fast_rate = 2.4 * 2500.0 ** jax.random.uniform(second, (HEADS,), jnp.float32)
    chosen = jax.random.bernoulli(third, 0.5, (HEADS,))
    return jnp.where(chosen, fast_rate, slow_rate)


def draw_decay_codes(key, part):
    first, second, third = jax.random.split(key, 3)
    base = jax.random.randint(first, (HEADS, TOKENS // TOK_DEV, TOK_DEV), 1, 4)
    factor = jax.random.randint(second, (HEADS, TOKENS // TOK_DEV, 1), 1, 3)
    codes = (base * factor).reshape(HEADS, TOKENS)
    spots = jax.random.randint(third, (3,), 0, TOKENS)
    places = jnp.arange(TOKENS, dtype=jnp.int32)
    struck = jnp.any(places[None, :] == spots[:, None], axis=0)
    return jnp.where(struck[None, :], 2 * TOKENS, codes).astype(jnp.int32)


def block_levels(stream_key, shape, pieces, smallest, high):
    level, own = 1.0, jax.random.fold_in(stream_key, 6)
    for axis_at, parts in pieces:
        heights = jnp.exp(jax.random.uniform(jax.random.fold_in(own, axis_at), (parts,), jnp.float32, smallest / len(pieces), high / len(pieces)))
        level = level * jnp.repeat(heights, shape[axis_at] // parts).reshape([-1 if axis == axis_at else 1 for axis in range(len(shape))])
    return level


def noise(stream_key, extent, scale, reach, pieces=(), kind=jnp.bfloat16):
    loudness = block_levels(stream_key, extent, pieces, -0.22, 0.18) if pieces else 1.0
    values = jax.random.normal(stream_key, extent, jnp.float32) * scale * loudness
    return jnp.minimum(jnp.maximum(values, -reach), reach).astype(kind)


def setup_inputs(seed: int = 0) -> dict:
    seeds = jax.random.split(jax.random.key(seed), 9)
    ssm_input = draw_ssm_input(jax.random.fold_in(seeds[8], 71), 0)
    gate_input = noise(seeds[1], (TOKENS, HEADS * HEAD_DIM), 1.5, 8.0, ((0, 16), (1, 2)))
    write_proj = noise(seeds[2], (TOKENS, STATE), TOK_DEV ** -0.5, 0.1875, ((0, 16),))
    read_proj = noise(seeds[3], (TOKENS, STATE), STATE ** -0.5, 0.5, ((0, 16),))
    decay_codes = draw_decay_codes(jax.random.fold_in(seeds[8], 71), 0)
    decay_rate = draw_decay_rate(jax.random.fold_in(seeds[8], 71), 0)
    skip_gain = jnp.clip(0.5 + 1.0 * jax.random.uniform(seeds[6], (HEADS,), jnp.float32) ** block_levels(seeds[6], (HEADS,), ((0, 2),), -0.2, 0.2), 0.5, 1.5)
    norm_gain = jnp.clip(1.0 + 0.1 * jax.random.normal(seeds[7], (HEADS * HEAD_DIM,), jnp.float32), 0.5, 1.5)
    return {"ssm_input": ssm_input, "gate_input": gate_input, "write_proj": write_proj, "read_proj": read_proj, "decay_codes": decay_codes, "decay_rate": decay_rate, "skip_gain": skip_gain, "norm_gain": norm_gain}


def reference(ssm_input, gate_input, write_proj, read_proj, decay_codes, decay_rate, skip_gain, norm_gain):
    block_count = TOKENS // GROUP
    log_decay = -(decay_codes.astype(jnp.float32) * decay_rate[:, None]) / (8.0 * TOKENS)
    cumulative = jnp.cumsum(log_decay.reshape(HEADS, block_count, GROUP), axis=2)
    x_blocks = ssm_input.reshape(block_count, GROUP, HEADS, HEAD_DIM)
    write_blocks = write_proj.reshape(block_count, GROUP, STATE)
    read_blocks = read_proj.reshape(block_count, GROUP, STATE)
    positions = jnp.arange(GROUP, dtype=jnp.int32)
    causal = positions[:, None] >= positions[None, :]

    def one_head(head_index):
        head_x = lax.dynamic_index_in_dim(x_blocks, head_index, 2, keepdims=False)
        head_cum = lax.dynamic_index_in_dim(cumulative, head_index, 0, keepdims=False)

        def block_step(running, block_items):
            x_part, write_part, read_part, cum_part = block_items
            scores = jnp.dot(read_part, write_part.T, preferred_element_type=jnp.float32)
            spread = cum_part[:, None] - cum_part[None, :]
            decay_mask = jnp.where(causal, jnp.exp(jnp.where(causal, spread, 0.0)), 0.0)
            mixing = (decay_mask * scores).astype(jnp.bfloat16)
            inner_out = jnp.dot(mixing, x_part, preferred_element_type=jnp.float32)
            carried = jnp.exp(cum_part)[:, None] * jnp.dot(read_part, running.astype(jnp.bfloat16), preferred_element_type=jnp.float32)
            weighted = (jnp.exp(cum_part[-1] - cum_part)[:, None] * x_part.astype(jnp.float32)).astype(jnp.bfloat16)
            block_state = jnp.dot(write_part.T, weighted, preferred_element_type=jnp.float32)
            running = jnp.exp(cum_part[-1]) * running + block_state
            return (running, inner_out + carried)
        start = jnp.zeros((STATE, HEAD_DIM), jnp.float32)
        _, head_out = lax.scan(block_step, start, (head_x, write_blocks, read_blocks, head_cum))
        return head_out
    head_out = lax.map(one_head, jnp.arange(HEADS, dtype=jnp.int32))
    ssm_out = head_out.transpose(1, 2, 0, 3).reshape(TOKENS, HEADS * HEAD_DIM)
    ssm_out = ssm_out + jnp.repeat(skip_gain, HEAD_DIM)[None, :] * ssm_input.astype(jnp.float32)
    gated_out = ssm_out * jax.nn.silu(gate_input.astype(jnp.float32))
    row_power = lax.optimization_barrier(jnp.mean(gated_out * gated_out, axis=1, keepdims=True))
    return (gated_out * lax.rsqrt(row_power + 1e-05) * norm_gain[None, :]).astype(jnp.bfloat16)
```

```python
import functools

import jax
import jax.numpy as jnp
from jax import lax
from jax.experimental import pallas as pl
from jax.experimental.pallas import tpu as pltpu
from jax.sharding import PartitionSpec as P

HEAD_DIM = 128
GROUP = 256
TEAM = 4
CHUNKS = 4
F32 = jnp.float32
MESH = pl.DeviceIdType.MESH


def dot(a, b, dims=((1,), (0,)), **kw):
    return lax.dot_general(a, b, (dims, ((), ())), preferred_element_type=F32, **kw)


def spread_lanes(columns, heads):
    rows = columns.shape[0]
    return jnp.concatenate(
        [jnp.broadcast_to(columns[:, h : h + 1], (rows, HEAD_DIM)) for h in range(heads)], axis=1
    )


def kernel(
    sections, groups, x_ref, g_ref, b_ref, c_ref, codes_ref, rate_ref, skip_ref, gain_ref, out_ref,
    cumc, cumr, ends, decay, total_decay, states, scores, y, sums, got, prefix, turns, enter_z,
    next_z, send_e, incoming, power, power_in, send1, recv1, send2, recv2, send3, recv3, send4, recv4,
):
    rows, width = x_ref.shape
    heads = codes_ref.shape[0]
    blocks = rows // GROUP
    part = heads // TEAM
    lanes = part * HEAD_DIM
    state = b_ref.shape[1]
    teams = sections // TEAM
    seq = lax.axis_index("seq")
    core = lax.axis_index("head")
    z, q = seq // TEAM, seq % TEAM
    mates = [z * TEAM + (q + i) % TEAM for i in range(1, TEAM)]
    step = state // CHUNKS

    barrier = pltpu.get_barrier_semaphore()
    for mate in mates:
        pl.semaphore_signal(barrier, inc=1, device_id={"seq": mate}, device_id_type=MESH)
    for i in range(1, groups):
        other = (core + i) % groups
        pl.semaphore_signal(barrier, inc=1, device_id={"head": other}, device_id_type=MESH)

    @pl.when(z > 0)
    def _():
        pl.semaphore_signal(barrier, inc=1, device_id={"seq": seq - TEAM}, device_id_type=MESH)

    @pl.when(z < teams - 1)
    def _():
        pl.semaphore_signal(barrier, inc=1, device_id={"seq": seq + TEAM}, device_id_type=MESH)

    def lane_slice(p):
        return pl.ds(pl.multiple_of(p * lanes, lanes), lanes)

    def row_slice(k):
        return pl.ds(pl.multiple_of(k * GROUP, GROUP), GROUP)

    t_at = lax.broadcasted_iota(jnp.int32, (GROUP, GROUP), 0)
    s_at = lax.broadcasted_iota(jnp.int32, (GROUP, GROUP), 1)
    upto = jnp.where(t_at <= s_at, 1.0, 0.0).astype(F32)
    for k in range(blocks):
        logs = -(codes_ref[:, k * GROUP : (k + 1) * GROUP].astype(F32) * rate_ref[...])
        logs = logs / (8.0 * rows * sections)
        cum = dot(logs, upto, precision=lax.Precision.HIGHEST)
        cum_t = cum.T
        for p in range(TEAM):
            cumc[k, p] = cum_t[:, p * part : (p + 1) * part]
            cumr[k, p, :part] = cum[p * part : (p + 1) * part]
        last = jnp.broadcast_to(cum[:, GROUP - 1 : GROUP], (heads, HEAD_DIM))
        for h in range(heads):
            ends[k, :, h * HEAD_DIM : (h + 1) * HEAD_DIM] = last[h : h + 1]
    decay[...] = jnp.exp(ends[...])
    total_decay[...] = jnp.exp(jnp.sum(ends[...], axis=0))

    def summarize(p, carry):
        at = lane_slice(p)
        run = jnp.zeros((state, lanes), F32)
        for k in range(blocks):
            col = cumc[k, p]
            tail = spread_lanes(jnp.exp(col[GROUP - 1 : GROUP] - col), part)
            own = slice(k * GROUP, (k + 1) * GROUP)
            weighted = (tail * x_ref[own, at].astype(F32)).astype(jnp.bfloat16)
            block_state = dot(b_ref[own, :], weighted, ((0,), (0,)))
            states[k, p] = block_state
            run = decay[k, :, at] * run + block_state
        sums[p, :state] = run
        sums[p, state:] = jnp.broadcast_to(total_decay[:, at], (8, lanes))
        return carry

    def to_owner(i):
        mate = (q + i) % TEAM
        return pltpu.make_async_remote_copy(
            src_ref=sums.at[mate], dst_ref=got.at[q], send_sem=send1.at[i - 1],
            recv_sem=recv1.at[i - 1], device_id={"seq": z * TEAM + mate}, device_id_type=MESH,
        )

    def first(i, carry):
        summarize((q + i) % TEAM, 0)

        @pl.when(i == 1)
        def _():
            behind = (z + teams - 1) // teams
            ahead = (2 * teams - 2 - z) // teams
            pl.semaphore_wait(barrier, TEAM - 1 + groups - 1 + behind + ahead)

        to_owner(i).start()
        return carry

    lax.fori_loop(1, TEAM, first, 0)
    summarize(q, 0)
    got[q] = sums[q]

    def score(k, carry):
        at = row_slice(k)
        full = dot(c_ref[at, :], b_ref[at, :], ((1,), (1,)))
        scores[k] = jnp.where(t_at >= s_at, full, 0.0)
        return carry

    lax.fori_loop(0, blocks, score, 0)
    half = GROUP // 2

    def inner(u, carry):
        k, p = u // TEAM, u % TEAM
        start = pl.multiple_of(k * GROUP, GROUP)
        for h in range(part):
            at = pl.ds(pl.multiple_of(p * lanes + h * HEAD_DIM, HEAD_DIM), HEAD_DIM)
            xs = x_ref[pl.ds(start, GROUP), at]
            skip = skip_ref[:, at]
            for r, cols in ((0, half), (half, GROUP)):
                spread = cumc[k, p, r : r + half, h : h + 1] - cumr[k, p, h : h + 1, :cols]
                mixing = jnp.exp(jnp.minimum(spread, 0.0)) * scores[k, r : r + half, :cols]
                got_out = dot(mixing.astype(jnp.bfloat16), xs[:cols])
                y[pl.ds(start + r, half), at] = got_out + skip * xs[r : r + half].astype(F32)
        return carry

    units = blocks * TEAM
    before = jnp.minimum(6 + 3 * z, units)
    lax.fori_loop(0, before, inner, 0)

    for i in range(1, TEAM):
        to_owner(i).wait()
    run = jnp.zeros((state, lanes), F32)
    through = jnp.ones((1, lanes), F32)
    for j in range(TEAM):
        prefix[j] = run
        turns[j] = jnp.broadcast_to(through, (8, lanes))
        run = got[j, state : state + 1] * run + got[j, :state]
        through = through * got[j, state : state + 1]
    prefix[TEAM] = run
    turns[TEAM] = jnp.broadcast_to(through, (8, lanes))

    @pl.when(z == 0)
    def _():
        enter_z[...] = jnp.zeros_like(enter_z)

    def along(c):
        at = pl.ds(pl.multiple_of(c * step, step), step)
        return pltpu.make_async_remote_copy(
            src_ref=next_z.at[at], dst_ref=enter_z.at[at], send_sem=send2.at[c],
            recv_sem=recv2.at[c], device_id={"seq": seq + TEAM}, device_id_type=MESH,
        )

    def to_mate(c, i):
        at = pl.ds(pl.multiple_of(c * step, step), step)
        mate = (q + i) % TEAM
        return pltpu.make_async_remote_copy(
            src_ref=send_e.at[mate, at], dst_ref=incoming.at[q, at], send_sem=send3.at[c, i - 1],
            recv_sem=recv3.at[c, i - 1], device_id={"seq": z * TEAM + mate}, device_id_type=MESH,
        )

    def hand_on(c, carry):
        at = pl.ds(pl.multiple_of(c * step, step), step)

        @pl.when(z > 0)
        def _():
            along(c).wait_recv()

        arrived = enter_z[at, :]

        @pl.when(z < teams - 1)
        def _():
            next_z[at, :] = turns[TEAM, :1] * arrived + prefix[TEAM, at, :]
            along(c).start()

        for j in range(TEAM):
            send_e[j, at, :] = turns[j, :1] * arrived + prefix[j, at, :]
        for i in range(1, TEAM):
            to_mate(c, i).start()
        return carry

    lax.fori_loop(0, CHUNKS, hand_on, 0)
    incoming[q] = send_e[q]
    lax.fori_loop(before, units, inner, 0)
    power[...] = jnp.zeros_like(power)

    def finish(p):
        at = lane_slice(p)

        def block(k, run):
            own = row_slice(k)
            read = dot(c_ref[own, :], run.astype(jnp.bfloat16))
            value = y[own, at] + spread_lanes(jnp.exp(cumc[k, p]), part) * read
            gate = g_ref[own, at].astype(F32)
            value = value * (gate / (1.0 + jnp.exp(-gate)))
            y[own, at] = value
            square = value * value
            folded = square[:, :HEAD_DIM]
            for h in range(1, part):
                folded = folded + square[:, h * HEAD_DIM : (h + 1) * HEAD_DIM]
            power[own, :] += folded
            return decay[k, :, at] * run + states[k, p]

        lax.fori_loop(0, blocks, block, incoming[p])

    finish(q)

    def rest(i, carry):
        for c in range(CHUNKS):
            to_mate(c, i).wait_recv()
        finish((q + TEAM - i) % TEAM)
        return carry

    lax.fori_loop(1, TEAM, rest, 0)

    def swap(i):
        return pltpu.make_async_remote_copy(
            src_ref=power, dst_ref=power_in.at[i - 1], send_sem=send4.at[i - 1],
            recv_sem=recv4.at[i - 1], device_id={"head": (core + i) % groups}, device_id_type=MESH,
        )

    for i in range(1, groups):
        swap(i).start()
    for c in range(CHUNKS):
        for i in range(1, TEAM):
            to_mate(c, i).wait_send()

    @pl.when(z < teams - 1)
    def _():
        for c in range(CHUNKS):
            along(c).wait_send()

    for i in range(1, groups):
        swap(i).wait()

    def norm(k, carry):
        own = row_slice(k)
        total = power[own, :]
        for i in range(groups - 1):
            total = total + power_in[i, own, :]
        mean = jnp.sum(total, axis=1, keepdims=True) / (groups * width)
        scale = lax.rsqrt(mean + 1e-05)
        for p in range(TEAM):
            at = slice(p * lanes, (p + 1) * lanes)
            out_ref[own, at] = (y[own, at] * scale * gain_ref[:, at]).astype(jnp.bfloat16)
        return carry

    lax.fori_loop(0, blocks, norm, 0)


def local(
    sections, groups, ssm_input, gate_input, write_proj, read_proj, decay_codes, decay_rate, skip_gain, norm_gain
):
    rows, width = ssm_input.shape
    heads = decay_rate.shape[0]
    state = write_proj.shape[1]
    blocks = rows // GROUP
    part = heads // TEAM
    lanes = part * HEAD_DIM
    in_vmem = pl.BlockSpec(memory_space=pltpu.VMEM)
    dma = pltpu.SemaphoreType.DMA
    return pl.pallas_call(
        functools.partial(kernel, sections, groups),
        out_shape=jax.ShapeDtypeStruct((rows, width), jnp.bfloat16),
        in_specs=[in_vmem] * 8,
        out_specs=in_vmem,
        scratch_shapes=[
            pltpu.VMEM((blocks, TEAM, GROUP, part), F32),
            pltpu.VMEM((blocks, TEAM, 8, GROUP), F32),
            pltpu.VMEM((blocks, 1, width), F32),
            pltpu.VMEM((blocks, 1, width), F32),
            pltpu.VMEM((1, width), F32),
            pltpu.VMEM((blocks, TEAM, state, lanes), F32),
            pltpu.VMEM((blocks, GROUP, GROUP), F32),
            pltpu.VMEM((rows, width), F32),
            pltpu.VMEM((TEAM, state + 8, lanes), F32),
            pltpu.VMEM((TEAM, state + 8, lanes), F32),
            pltpu.VMEM((TEAM + 1, state, lanes), F32),
            pltpu.VMEM((TEAM + 1, 8, lanes), F32),
            pltpu.VMEM((state, lanes), F32),
            pltpu.VMEM((state, lanes), F32),
            pltpu.VMEM((TEAM, state, lanes), F32),
            pltpu.VMEM((TEAM, state, lanes), F32),
            pltpu.VMEM((rows, HEAD_DIM), F32),
            pltpu.VMEM((groups - 1, rows, HEAD_DIM), F32),
            dma((TEAM - 1,)),
            dma((TEAM - 1,)),
            dma((CHUNKS,)),
            dma((CHUNKS,)),
            dma((CHUNKS, TEAM - 1)),
            dma((CHUNKS, TEAM - 1)),
            dma((groups - 1,)),
            dma((groups - 1,)),
        ],
        compiler_params=pltpu.CompilerParams(
            collective_id=0, has_side_effects=True, vmem_limit_bytes=56 * 1024 * 1024
        ),
    )(
        ssm_input, gate_input, write_proj, read_proj, decay_codes, decay_rate[:, None],
        jnp.repeat(skip_gain, HEAD_DIM)[None, :], norm_gain[None, :],
    )


def solution(mesh):
    placed = (
        P("seq", "head"),
        P("seq", "head"),
        P("seq", None),
        P("seq", None),
        P("head", "seq"),
        P("head"),
        P("head"),
        P("head"),
    )
    return jax.shard_map(
        functools.partial(local, mesh.shape["seq"], mesh.shape["head"]),
        mesh=mesh, in_specs=placed, out_specs=P("seq", "head"), check_vma=False,
    )
```

```python
import functools

import jax
import jax.numpy as jnp
from jax import lax
from jax.experimental import pallas as pl
from jax.experimental.pallas import tpu as pltpu
from jax.sharding import PartitionSpec as P

HEAD_DIM = 128
GROUP = 256
TEAM = 4
CHUNKS = 4
F32 = jnp.float32
MESH = pl.DeviceIdType.MESH


def dot(a, b, dims=((1,), (0,)), **kw):
    return lax.dot_general(a, b, (dims, ((), ())), preferred_element_type=F32, **kw)


def spread_lanes(columns, heads):
    rows = columns.shape[0]
    return jnp.concatenate(
        [jnp.broadcast_to(columns[:, h : h + 1], (rows, HEAD_DIM)) for h in range(heads)], axis=1
    )


def kernel(
    sections, groups, x_hbm, g_hbm, b_ref, c_ref, codes_ref, rate_ref, skip_ref, out_hbm, scale_ref,
    x_ref, g_ref, gated, carry_gain, skip_row,    cumc, cumr, ends, decay, total_decay, states, scores, y, sums, got, prefix, turns, enter_z,
    next_z, send_e, incoming, power, power_in, send1, recv1, send2, recv2, send3, recv3, send4, recv4,
    load_x, load_g, store,
):
    rows, width = x_hbm.shape
    heads = codes_ref.shape[0]
    blocks = rows // GROUP
    part = heads // TEAM
    lanes = part * HEAD_DIM
    state = b_ref.shape[1]
    teams = sections // TEAM
    seq = lax.axis_index("seq")
    core = lax.axis_index("head")
    z, q = seq // TEAM, seq % TEAM
    mates = [z * TEAM + (q + i) % TEAM for i in range(1, TEAM)]
    step = state // CHUNKS

    def lane_slice(p):
        return pl.ds(pl.multiple_of(p * lanes, lanes), lanes)

    def row_slice(k):
        return pl.ds(pl.multiple_of(k * GROUP, GROUP), GROUP)

    def fetch_x(i):
        at = lane_slice((q + i) % TEAM)
        return pltpu.make_async_copy(x_hbm.at[:, at], x_ref.at[:, at], load_x.at[i % TEAM])

    def put(p):
        at = lane_slice(p)
        return pltpu.make_async_copy(gated.at[:, at], out_hbm.at[:, at], store.at[p])

    fetch_g = pltpu.make_async_copy(g_hbm, g_ref, load_g)
    for i in range(1, TEAM + 1):
        fetch_x(i).start()
    fetch_g.start()

    barrier = pltpu.get_barrier_semaphore()
    for mate in mates:
        pl.semaphore_signal(barrier, inc=1, device_id={"seq": mate}, device_id_type=MESH)
    for i in range(1, groups):
        other = (core + i) % groups
        pl.semaphore_signal(barrier, inc=1, device_id={"head": other}, device_id_type=MESH)

    @pl.when(z > 0)
    def _():
        pl.semaphore_signal(barrier, inc=1, device_id={"seq": seq - TEAM}, device_id_type=MESH)

    @pl.when(z < teams - 1)
    def _():
        pl.semaphore_signal(barrier, inc=1, device_id={"seq": seq + TEAM}, device_id_type=MESH)

    t_at = lax.broadcasted_iota(jnp.int32, (GROUP, GROUP), 0)
    s_at = lax.broadcasted_iota(jnp.int32, (GROUP, GROUP), 1)
    upto = jnp.where(t_at <= s_at, 1.0, 0.0).astype(F32)
    own_row = lax.broadcasted_iota(jnp.int32, (heads, heads), 0)
    own_col = lax.broadcasted_iota(jnp.int32, (heads, heads), 1)
    rate = jnp.sum(jnp.where(own_row == own_col, rate_ref[...], 0.0), axis=1, keepdims=True)
    skip_row[...] = spread_lanes(skip_ref[...], heads)
    for k in range(blocks):
        logs = -(codes_ref[:, k * GROUP : (k + 1) * GROUP].astype(F32) * rate)
        logs = logs / (8.0 * rows * sections)
        cum = dot(logs, upto, precision=lax.Precision.HIGHEST)
        cum_t = cum.T
        for p in range(TEAM):
            cumc[k, p] = cum_t[:, p * part : (p + 1) * part]
            cumr[k, p, :part] = cum[p * part : (p + 1) * part]
        last = jnp.broadcast_to(cum[:, GROUP - 1 : GROUP], (heads, HEAD_DIM))
        for h in range(heads):
            ends[k, :, h * HEAD_DIM : (h + 1) * HEAD_DIM] = last[h : h + 1]
    decay[...] = jnp.exp(ends[...])
    total_decay[...] = jnp.exp(jnp.sum(ends[...], axis=0))

    def summarize(p, carry):
        at = lane_slice(p)
        run = jnp.zeros((state, lanes), F32)
        for k in range(blocks):
            col = cumc[k, p]
            tail = spread_lanes(jnp.exp(col[GROUP - 1 : GROUP] - col), part)
            own = slice(k * GROUP, (k + 1) * GROUP)
            weighted = (tail * x_ref[own, at].astype(F32)).astype(jnp.bfloat16)
            block_state = dot(b_ref[own, :], weighted, ((0,), (0,)))
            states[k, p] = block_state
            run = decay[k, :, at] * run + block_state
        sums[p, :state] = run
        sums[p, state:] = jnp.broadcast_to(total_decay[:, at], (8, lanes))
        return carry

    def to_owner(i):
        mate = (q + i) % TEAM
        return pltpu.make_async_remote_copy(
            src_ref=sums.at[mate], dst_ref=got.at[q], send_sem=send1.at[i - 1],
            recv_sem=recv1.at[i - 1], device_id={"seq": z * TEAM + mate}, device_id_type=MESH,
        )

    def first(i, carry):
        fetch_x(i).wait()
        summarize((q + i) % TEAM, 0)

        @pl.when(i == 1)
        def _():
            behind = (z + teams - 1) // teams
            ahead = (2 * teams - 2 - z) // teams
            pl.semaphore_wait(barrier, TEAM - 1 + groups - 1 + behind + ahead)

        to_owner(i).start()
        return carry

    lax.fori_loop(1, TEAM, first, 0)
    fetch_x(TEAM).wait()
    summarize(q, 0)
    got[q] = sums[q]

    def score(k, carry):
        at = row_slice(k)
        full = dot(c_ref[at, :], b_ref[at, :], ((1,), (1,)))
        scores[k] = jnp.where(t_at >= s_at, full, 0.0)
        return carry

    lax.fori_loop(0, blocks, score, 0)
    half = GROUP // 2
    fetch_g.wait()

    def inner(u, carry):
        k, p = u // TEAM, u % TEAM
        start = pl.multiple_of(k * GROUP, GROUP)
        reach = jnp.exp(cumc[k, p])
        for h in range(part):
            at = pl.ds(pl.multiple_of(p * lanes + h * HEAD_DIM, HEAD_DIM), HEAD_DIM)
            xs = x_ref[pl.ds(start, GROUP), at]
            skip = skip_row[:, at]
            for r, cols in ((0, half), (half, GROUP)):
                spread = cumc[k, p, r : r + half, h : h + 1] - cumr[k, p, h : h + 1, :cols]
                mixing = jnp.exp(jnp.minimum(spread, 0.0)) * scores[k, r : r + half, :cols]
                got_out = dot(mixing.astype(jnp.bfloat16), xs[:cols])
                here = pl.ds(pl.multiple_of(start + r, half), half)
                gate = g_ref[here, at].astype(F32)
                gate = gate * (0.5 * jnp.tanh(0.5 * gate) + 0.5)
                y[here, at] = (got_out + skip * xs[r : r + half].astype(F32)) * gate
                carry_gain[here, at] = reach[r : r + half, h : h + 1] * gate
        return carry

    units = blocks * TEAM
    before = jnp.minimum(6 + 3 * z, units)
    lax.fori_loop(0, before, inner, 0)

    for i in range(1, TEAM):
        to_owner(i).wait()
    run = jnp.zeros((state, lanes), F32)
    through = jnp.ones((1, lanes), F32)
    for j in range(TEAM):
        prefix[j] = run
        turns[j] = jnp.broadcast_to(through, (8, lanes))
        run = got[j, state : state + 1] * run + got[j, :state]
        through = through * got[j, state : state + 1]
    prefix[TEAM] = run
    turns[TEAM] = jnp.broadcast_to(through, (8, lanes))

    @pl.when(z == 0)
    def _():
        enter_z[...] = jnp.zeros_like(enter_z)

    def along(c):
        at = pl.ds(pl.multiple_of(c * step, step), step)
        return pltpu.make_async_remote_copy(
            src_ref=next_z.at[at], dst_ref=enter_z.at[at], send_sem=send2.at[c],
            recv_sem=recv2.at[c], device_id={"seq": seq + TEAM}, device_id_type=MESH,
        )

    def to_mate(c, i):
        at = pl.ds(pl.multiple_of(c * step, step), step)
        mate = (q + i) % TEAM
        return pltpu.make_async_remote_copy(
            src_ref=send_e.at[mate, at], dst_ref=incoming.at[q, at], send_sem=send3.at[c, i - 1],
            recv_sem=recv3.at[c, i - 1], device_id={"seq": z * TEAM + mate}, device_id_type=MESH,
        )

    def hand_on(c, carry):
        at = pl.ds(pl.multiple_of(c * step, step), step)

        @pl.when(z > 0)
        def _():
            along(c).wait_recv()

        arrived = enter_z[at, :]

        @pl.when(z < teams - 1)
        def _():
            next_z[at, :] = turns[TEAM, :1] * arrived + prefix[TEAM, at, :]
            along(c).start()

        for j in range(TEAM):
            send_e[j, at, :] = turns[j, :1] * arrived + prefix[j, at, :]
        for i in range(1, TEAM):
            to_mate(c, i).start()
        return carry

    lax.fori_loop(0, CHUNKS, hand_on, 0)
    incoming[q] = send_e[q]
    lax.fori_loop(before, units, inner, 0)
    power[...] = jnp.zeros_like(power)

    def finish(p):
        at = lane_slice(p)

        def block(k, run):
            own = row_slice(k)
            read = dot(c_ref[own, :], run.astype(jnp.bfloat16))
            value = y[own, at] + carry_gain[own, at] * read
            gated[own, at] = value.astype(jnp.bfloat16)
            square = value * value
            folded = square[:, :HEAD_DIM]
            for h in range(1, part):
                folded = folded + square[:, h * HEAD_DIM : (h + 1) * HEAD_DIM]
            power[own, :] += folded
            return decay[k, :, at] * run + states[k, p]

        lax.fori_loop(0, blocks, block, incoming[p])
        put(p).start()

    finish(q)

    def rest(i, carry):
        for c in range(CHUNKS):
            to_mate(c, i).wait_recv()
        finish((q + TEAM - i) % TEAM)
        return carry

    lax.fori_loop(1, TEAM, rest, 0)

    def swap(i):
        return pltpu.make_async_remote_copy(
            src_ref=power, dst_ref=power_in.at[i - 1], send_sem=send4.at[i - 1],
            recv_sem=recv4.at[i - 1], device_id={"head": (core + i) % groups}, device_id_type=MESH,
        )

    for i in range(1, groups):
        swap(i).start()
    for c in range(CHUNKS):
        for i in range(1, TEAM):
            to_mate(c, i).wait_send()

    @pl.when(z < teams - 1)
    def _():
        for c in range(CHUNKS):
            along(c).wait_send()

    for i in range(1, groups):
        swap(i).wait()

    def norm(k, carry):
        own = row_slice(k)
        total = power[own, :]
        for i in range(groups - 1):
            total = total + power_in[i, own, :]
        mean = jnp.sum(total, axis=1, keepdims=True) / (groups * width)
        scale_ref[own, :] = jnp.broadcast_to(lax.rsqrt(mean + 1e-05), (GROUP, HEAD_DIM))
        return carry

    lax.fori_loop(0, blocks, norm, 0)
    for p in range(TEAM):
        put(p).wait()


def apply_norm(gated_ref, scale_ref, gain_ref, out_ref):
    scale = scale_ref[...]
    for at in range(0, gated_ref.shape[1], HEAD_DIM):
        own = slice(at, at + HEAD_DIM)
        value = gated_ref[:, own].astype(F32) * scale * gain_ref[:, own]
        out_ref[:, own] = value.astype(jnp.bfloat16)


def local(
    sections, groups, ssm_input, gate_input, write_proj, read_proj, decay_codes, decay_rate, skip_gain, norm_gain
):
    rows, width = ssm_input.shape
    heads = decay_rate.shape[0]
    state = write_proj.shape[1]
    blocks = rows // GROUP
    part = heads // TEAM
    lanes = part * HEAD_DIM
    in_vmem = pl.BlockSpec(memory_space=pltpu.VMEM)
    dma = pltpu.SemaphoreType.DMA
    in_place = pl.BlockSpec(memory_space=pl.ANY)
    gated, scale = pl.pallas_call(
        functools.partial(kernel, sections, groups),
        out_shape=(
            jax.ShapeDtypeStruct((rows, width), jnp.bfloat16),
            jax.ShapeDtypeStruct((rows, HEAD_DIM), F32),
        ),
        in_specs=[in_place] * 2 + [in_vmem] * 5,
        out_specs=(in_place, in_vmem),
        scratch_shapes=[
            pltpu.VMEM((rows, width), jnp.bfloat16),
            pltpu.VMEM((rows, width), jnp.bfloat16),
            pltpu.VMEM((rows, width), jnp.bfloat16),
            pltpu.VMEM((rows, width), F32),
            pltpu.VMEM((1, width), F32),
            pltpu.VMEM((blocks, TEAM, GROUP, part), F32),
            pltpu.VMEM((blocks, TEAM, 8, GROUP), F32),
            pltpu.VMEM((blocks, 1, width), F32),
            pltpu.VMEM((blocks, 1, width), F32),
            pltpu.VMEM((1, width), F32),
            pltpu.VMEM((blocks, TEAM, state, lanes), F32),
            pltpu.VMEM((blocks, GROUP, GROUP), F32),
            pltpu.VMEM((rows, width), F32),
            pltpu.VMEM((TEAM, state + 8, lanes), F32),
            pltpu.VMEM((TEAM, state + 8, lanes), F32),
            pltpu.VMEM((TEAM + 1, state, lanes), F32),
            pltpu.VMEM((TEAM + 1, 8, lanes), F32),
            pltpu.VMEM((state, lanes), F32),
            pltpu.VMEM((state, lanes), F32),
            pltpu.VMEM((TEAM, state, lanes), F32),
            pltpu.VMEM((TEAM, state, lanes), F32),
            pltpu.VMEM((rows, HEAD_DIM), F32),
            pltpu.VMEM((groups - 1, rows, HEAD_DIM), F32),
            dma((TEAM - 1,)),
            dma((TEAM - 1,)),
            dma((CHUNKS,)),
            dma((CHUNKS,)),
            dma((CHUNKS, TEAM - 1)),
            dma((CHUNKS, TEAM - 1)),
            dma((groups - 1,)),
            dma((groups - 1,)),
            dma((TEAM,)),
            dma,
            dma((TEAM,)),
        ],
        compiler_params=pltpu.CompilerParams(
            collective_id=0, has_side_effects=True, vmem_limit_bytes=56 * 1024 * 1024
        ),
    )(
        ssm_input, gate_input, write_proj, read_proj, decay_codes, decay_rate[None, :],
        skip_gain[None, :],
    )
    tile = GROUP // 2
    return pl.pallas_call(
        apply_norm,
        grid=(rows // tile,),
        out_shape=jax.ShapeDtypeStruct((rows, width), jnp.bfloat16),
        in_specs=[
            pl.BlockSpec((tile, width), lambda i: (i, 0)),
            pl.BlockSpec((tile, HEAD_DIM), lambda i: (i, 0)),
            pl.BlockSpec((1, width), lambda i: (0, 0)),
        ],
        out_specs=pl.BlockSpec((tile, width), lambda i: (i, 0)),
        compiler_params=pltpu.CompilerParams(vmem_limit_bytes=56 * 1024 * 1024),
    )(gated, scale, norm_gain[None, :])


def solution(mesh):
    placed = (
        P("seq", "head"),
        P("seq", "head"),
        P("seq", None),
        P("seq", None),
        P("head", "seq"),
        P("head"),
        P("head"),
        P("head"),
    )
    return jax.shard_map(
        functools.partial(local, mesh.shape["seq"], mesh.shape["head"]),
        mesh=mesh, in_specs=placed, out_specs=P("seq", "head"), check_vma=False,
    )
```

```python
import functools

import jax
import jax.numpy as jnp
from jax import lax
from jax.experimental import pallas as pl
from jax.experimental.pallas import tpu as pltpu
from jax.sharding import PartitionSpec as P

HEAD_DIM = 128
GROUP = 256
TEAM = 4
CHUNKS = 4
F32 = jnp.float32
MESH = pl.DeviceIdType.MESH


def dot(a, b, dims=((1,), (0,)), **kw):
    return lax.dot_general(a, b, (dims, ((), ())), preferred_element_type=F32, **kw)


def spread_lanes(columns, heads):
    rows = columns.shape[0]
    return jnp.concatenate(
        [jnp.broadcast_to(columns[:, h : h + 1], (rows, HEAD_DIM)) for h in range(heads)], axis=1
    )


def kernel(
    sections, groups, x_hbm, g_hbm, b_ref, c_ref, codes_ref, rate_ref, skip_ref, out_hbm, scale_ref,
    x_ref, g_ref, gated, carry_gain, skip_row,    cumc, cumr, ends, decay, total_decay, states, scores, y, sums, got, prefix, turns, enter_z,
    next_z, send_e, incoming, power, power_in, send1, recv1, send2, recv2, send3, recv3, send4, recv4,
    load_x, load_g, store,
):
    rows, width = x_hbm.shape
    heads = codes_ref.shape[0]
    blocks = rows // GROUP
    part = heads // TEAM
    lanes = part * HEAD_DIM
    state = b_ref.shape[1]
    teams = sections // TEAM
    seq = lax.axis_index("seq")
    core = lax.axis_index("head")
    z, q = seq // TEAM, seq % TEAM
    mates = [z * TEAM + (q + i) % TEAM for i in range(1, TEAM)]
    step = state // CHUNKS

    def lane_slice(p):
        return pl.ds(pl.multiple_of(p * lanes, lanes), lanes)

    def row_slice(k):
        return pl.ds(pl.multiple_of(k * GROUP, GROUP), GROUP)

    def fetch_x(i):
        at = lane_slice((q + i) % TEAM)
        return pltpu.make_async_copy(x_hbm.at[:, at], x_ref.at[:, at], load_x.at[i % TEAM])

    def put(p):
        at = lane_slice(p)
        return pltpu.make_async_copy(gated.at[:, at], out_hbm.at[:, at], store.at[p])

    fetch_g = pltpu.make_async_copy(g_hbm, g_ref, load_g)
    for i in range(1, TEAM + 1):
        fetch_x(i).start()
    fetch_g.start()

    barrier = pltpu.get_barrier_semaphore()
    for mate in mates:
        pl.semaphore_signal(barrier, inc=1, device_id={"seq": mate}, device_id_type=MESH)
    for i in range(1, groups):
        other = (core + i) % groups
        pl.semaphore_signal(barrier, inc=1, device_id={"head": other}, device_id_type=MESH)

    @pl.when(z > 0)
    def _():
        pl.semaphore_signal(barrier, inc=1, device_id={"seq": seq - TEAM}, device_id_type=MESH)

    @pl.when(z < teams - 1)
    def _():
        pl.semaphore_signal(barrier, inc=1, device_id={"seq": seq + TEAM}, device_id_type=MESH)

    t_at = lax.broadcasted_iota(jnp.int32, (GROUP, GROUP), 0)
    s_at = lax.broadcasted_iota(jnp.int32, (GROUP, GROUP), 1)
    upto = jnp.where(t_at <= s_at, 1.0, 0.0).astype(F32)
    own_row = lax.broadcasted_iota(jnp.int32, (heads, heads), 0)
    own_col = lax.broadcasted_iota(jnp.int32, (heads, heads), 1)
    rate = jnp.sum(jnp.where(own_row == own_col, rate_ref[...], 0.0), axis=1, keepdims=True)
    skip_row[...] = spread_lanes(skip_ref[...], heads)
    for k in range(blocks):
        logs = -(codes_ref[:, k * GROUP : (k + 1) * GROUP].astype(F32) * rate)
        logs = logs / (8.0 * rows * sections)
        cum = dot(logs, upto, precision=lax.Precision.HIGHEST)
        cum_t = cum.T
        for p in range(TEAM):
            cumc[k, p] = cum_t[:, p * part : (p + 1) * part]
            cumr[k, p, :part] = cum[p * part : (p + 1) * part]
        last = jnp.broadcast_to(cum[:, GROUP - 1 : GROUP], (heads, HEAD_DIM))
        for h in range(heads):
            ends[k, :, h * HEAD_DIM : (h + 1) * HEAD_DIM] = last[h : h + 1]
    decay[...] = jnp.exp(ends[...])
    total_decay[...] = jnp.exp(jnp.sum(ends[...], axis=0))

    def summarize(p, carry):
        at = lane_slice(p)
        run = jnp.zeros((state, lanes), F32)
        for k in range(blocks):
            col = cumc[k, p]
            tail = spread_lanes(jnp.exp(col[GROUP - 1 : GROUP] - col), part)
            own = slice(k * GROUP, (k + 1) * GROUP)
            weighted = (tail * x_ref[own, at].astype(F32)).astype(jnp.bfloat16)
            block_state = dot(b_ref[own, :], weighted, ((0,), (0,)))
            states[k, p] = block_state
            run = decay[k, :, at] * run + block_state
        sums[p, :state] = run
        sums[p, state:] = jnp.broadcast_to(total_decay[:, at], (8, lanes))
        return carry

    def to_owner(i):
        mate = (q + i) % TEAM
        return pltpu.make_async_remote_copy(
            src_ref=sums.at[mate], dst_ref=got.at[q], send_sem=send1.at[i - 1],
            recv_sem=recv1.at[i - 1], device_id={"seq": z * TEAM + mate}, device_id_type=MESH,
        )

    def first(i, carry):
        fetch_x(i).wait()
        summarize((q + i) % TEAM, 0)

        @pl.when(i == 1)
        def _():
            behind = (z + teams - 1) // teams
            ahead = (2 * teams - 2 - z) // teams
            pl.semaphore_wait(barrier, TEAM - 1 + groups - 1 + behind + ahead)

        to_owner(i).start()
        return carry

    lax.fori_loop(1, TEAM, first, 0)
    fetch_x(TEAM).wait()
    summarize(q, 0)
    got[q] = sums[q]

    def score(k, carry):
        at = row_slice(k)
        full = dot(c_ref[at, :], b_ref[at, :], ((1,), (1,)))
        scores[k] = jnp.where(t_at >= s_at, full, 0.0)
        return carry

    lax.fori_loop(0, blocks, score, 0)
    half = GROUP // 2
    fetch_g.wait()

    def inner(u, carry):
        k, p = u // TEAM, u % TEAM
        start = pl.multiple_of(k * GROUP, GROUP)
        reach = jnp.exp(cumc[k, p])
        for h in range(part):
            at = pl.ds(pl.multiple_of(p * lanes + h * HEAD_DIM, HEAD_DIM), HEAD_DIM)
            xs = x_ref[pl.ds(start, GROUP), at]
            skip = skip_row[:, at]
            for r, cols in ((0, half), (half, GROUP)):
                spread = cumc[k, p, r : r + half, h : h + 1] - cumr[k, p, h : h + 1, :cols]
                mixing = jnp.exp(jnp.minimum(spread, 0.0)) * scores[k, r : r + half, :cols]
                got_out = dot(mixing.astype(jnp.bfloat16), xs[:cols])
                here = pl.ds(pl.multiple_of(start + r, half), half)
                gate = g_ref[here, at].astype(F32)
                gate = gate * (0.5 * jnp.tanh(0.5 * gate) + 0.5)
                y[here, at] = (got_out + skip * xs[r : r + half].astype(F32)) * gate
                carry_gain[here, at] = reach[r : r + half, h : h + 1] * gate
        return carry

    units = blocks * TEAM
    before = jnp.minimum(6 + 2 * z, units)
    lax.fori_loop(0, before, inner, 0)

    for i in range(1, TEAM):
        to_owner(i).wait()
    run = jnp.zeros((state, lanes), F32)
    through = jnp.ones((1, lanes), F32)
    for j in range(TEAM):
        prefix[j] = run
        turns[j] = jnp.broadcast_to(through, (8, lanes))
        run = got[j, state : state + 1] * run + got[j, :state]
        through = through * got[j, state : state + 1]
    prefix[TEAM] = run
    turns[TEAM] = jnp.broadcast_to(through, (8, lanes))

    @pl.when(z == 0)
    def _():
        enter_z[...] = jnp.zeros_like(enter_z)

    def along(c):
        at = pl.ds(pl.multiple_of(c * step, step), step)
        return pltpu.make_async_remote_copy(
            src_ref=next_z.at[at], dst_ref=enter_z.at[at], send_sem=send2.at[c],
            recv_sem=recv2.at[c], device_id={"seq": seq + TEAM}, device_id_type=MESH,
        )

    def to_mate(c, i):
        at = pl.ds(pl.multiple_of(c * step, step), step)
        mate = (q + i) % TEAM
        return pltpu.make_async_remote_copy(
            src_ref=send_e.at[mate, at], dst_ref=incoming.at[q, at], send_sem=send3.at[c, i - 1],
            recv_sem=recv3.at[c, i - 1], device_id={"seq": z * TEAM + mate}, device_id_type=MESH,
        )

    def hand_on(c, carry):
        at = pl.ds(pl.multiple_of(c * step, step), step)

        @pl.when(z > 0)
        def _():
            along(c).wait_recv()

        arrived = enter_z[at, :]

        @pl.when(z < teams - 1)
        def _():
            next_z[at, :] = turns[TEAM, :1] * arrived + prefix[TEAM, at, :]
            along(c).start()

        for j in range(TEAM):
            send_e[j, at, :] = turns[j, :1] * arrived + prefix[j, at, :]
        for i in range(1, TEAM):
            to_mate(c, i).start()
        return carry

    lax.fori_loop(0, CHUNKS, hand_on, 0)
    incoming[q] = send_e[q]
    lax.fori_loop(before, units, inner, 0)
    power[...] = jnp.zeros_like(power)

    def finish(p):
        at = lane_slice(p)

        def block(k, run):
            own = row_slice(k)
            read = dot(c_ref[own, :], run.astype(jnp.bfloat16))
            value = y[own, at] + carry_gain[own, at] * read
            gated[own, at] = value.astype(jnp.bfloat16)
            square = value * value
            folded = square[:, :HEAD_DIM]
            for h in range(1, part):
                folded = folded + square[:, h * HEAD_DIM : (h + 1) * HEAD_DIM]
            power[own, :] += folded
            return decay[k, :, at] * run + states[k, p]

        lax.fori_loop(0, blocks, block, incoming[p])
        put(p).start()

    finish(q)

    def rest(i, carry):
        for c in range(CHUNKS):
            to_mate(c, i).wait_recv()
        finish((q + TEAM - i) % TEAM)
        return carry

    lax.fori_loop(1, TEAM, rest, 0)

    def swap(i):
        return pltpu.make_async_remote_copy(
            src_ref=power, dst_ref=power_in.at[i - 1], send_sem=send4.at[i - 1],
            recv_sem=recv4.at[i - 1], device_id={"head": (core + i) % groups}, device_id_type=MESH,
        )

    for i in range(1, groups):
        swap(i).start()
    for c in range(CHUNKS):
        for i in range(1, TEAM):
            to_mate(c, i).wait_send()

    @pl.when(z < teams - 1)
    def _():
        for c in range(CHUNKS):
            along(c).wait_send()

    for i in range(1, groups):
        swap(i).wait()

    def norm(k, carry):
        own = row_slice(k)
        total = power[own, :]
        for i in range(groups - 1):
            total = total + power_in[i, own, :]
        mean = jnp.sum(total, axis=1, keepdims=True) / (groups * width)
        scale_ref[own, :] = jnp.broadcast_to(lax.rsqrt(mean + 1e-05), (GROUP, HEAD_DIM))
        return carry

    lax.fori_loop(0, blocks, norm, 0)
    for p in range(TEAM):
        put(p).wait()


def local(
    sections, groups, ssm_input, gate_input, write_proj, read_proj, decay_codes, decay_rate, skip_gain, norm_gain
):
    rows, width = ssm_input.shape
    heads = decay_rate.shape[0]
    state = write_proj.shape[1]
    blocks = rows // GROUP
    part = heads // TEAM
    lanes = part * HEAD_DIM
    in_vmem = pl.BlockSpec(memory_space=pltpu.VMEM)
    dma = pltpu.SemaphoreType.DMA
    in_place = pl.BlockSpec(memory_space=pl.ANY)
    gated, scale = pl.pallas_call(
        functools.partial(kernel, sections, groups),
        out_shape=(
            jax.ShapeDtypeStruct((rows, width), jnp.bfloat16),
            jax.ShapeDtypeStruct((rows, HEAD_DIM), F32),
        ),
        in_specs=[in_place] * 2 + [in_vmem] * 5,
        out_specs=(in_place, in_vmem),
        scratch_shapes=[
            pltpu.VMEM((rows, width), jnp.bfloat16),
            pltpu.VMEM((rows, width), jnp.bfloat16),
            pltpu.VMEM((rows, width), jnp.bfloat16),
            pltpu.VMEM((rows, width), F32),
            pltpu.VMEM((1, width), F32),
            pltpu.VMEM((blocks, TEAM, GROUP, part), F32),
            pltpu.VMEM((blocks, TEAM, 8, GROUP), F32),
            pltpu.VMEM((blocks, 1, width), F32),
            pltpu.VMEM((blocks, 1, width), F32),
            pltpu.VMEM((1, width), F32),
            pltpu.VMEM((blocks, TEAM, state, lanes), F32),
            pltpu.VMEM((blocks, GROUP, GROUP), F32),
            pltpu.VMEM((rows, width), F32),
            pltpu.VMEM((TEAM, state + 8, lanes), F32),
            pltpu.VMEM((TEAM, state + 8, lanes), F32),
            pltpu.VMEM((TEAM + 1, state, lanes), F32),
            pltpu.VMEM((TEAM + 1, 8, lanes), F32),
            pltpu.VMEM((state, lanes), F32),
            pltpu.VMEM((state, lanes), F32),
            pltpu.VMEM((TEAM, state, lanes), F32),
            pltpu.VMEM((TEAM, state, lanes), F32),
            pltpu.VMEM((rows, HEAD_DIM), F32),
            pltpu.VMEM((groups - 1, rows, HEAD_DIM), F32),
            dma((TEAM - 1,)),
            dma((TEAM - 1,)),
            dma((CHUNKS,)),
            dma((CHUNKS,)),
            dma((CHUNKS, TEAM - 1)),
            dma((CHUNKS, TEAM - 1)),
            dma((groups - 1,)),
            dma((groups - 1,)),
            dma((TEAM,)),
            dma,
            dma((TEAM,)),
        ],
        compiler_params=pltpu.CompilerParams(
            collective_id=0, has_side_effects=True, vmem_limit_bytes=56 * 1024 * 1024
        ),
    )(
        ssm_input, gate_input, write_proj, read_proj, decay_codes, decay_rate[None, :],
        skip_gain[None, :],
    )
    value = gated.astype(F32) * scale[:, :1] * norm_gain[None, :]
    return value.astype(jnp.bfloat16)


def solution(mesh):
    placed = (
        P("seq", "head"),
        P("seq", "head"),
        P("seq", None),
        P("seq", None),
        P("head", "seq"),
        P("head"),
        P("head"),
        P("head"),
    )
    return jax.shard_map(
        functools.partial(local, mesh.shape["seq"], mesh.shape["head"]),
        mesh=mesh, in_specs=placed, out_specs=P("seq", "head"), check_vma=False,
    )
```
